256 devices in a mesh: row: 32 (over z, y_hi, core), rep: 8 (over y_lo, x).
Axes of the slice: x: 4, y: 4 (y_hi: 2, y_lo: 2; y = y_hi * 2 + y_lo), z: 8, core: 2. Of those that a mesh axis runs over, the one named last changes fastest.
Arguments:
- features: bfloat16 [32768, 256], P(('row', 'rep')), may hold values from -6 to 6
- weight: bfloat16 [256, 256], replicated, may hold values from -0.375 to 0.375
- tiles: bfloat16 [32, 8, 128, 128, 128], P('row', 'rep'), as said below
- tile_source: int32 [32, 8, 128], P('row', 'rep'), may hold values from 0 to 31, as said below
- tile_target: int32 [32, 8, 128], P('row', 'rep'), may hold values from 0 to 7, as said below
- live_tiles: int32 [32, 8], P('row', 'rep'), may hold values from 16 to 128, as said below
- wanted: int32 [32, 8, 32, 1], P('row', 'rep'), may hold values from 0 to 7
Outputs:
- aggregate: bfloat16 [32768, 256], P(('row', 'rep'))
The draws below stay inside these ranges and needn't reach their ends.
Inputs may be any that keep to these rules, and one draw needn't show every extreme that they name: `live_tiles`: device (0, 0) holds all 128 slots filled; each count is max(1, 128 // m) for m of 1, 2, 4 or 8. Within one device the pairs (tile_source, tile_target) of its slots are all different. Within one device the pairs (tile_source, tile_target) of its slots are all different. `tiles`: Nonnegative.
All inputs are finite; a program needn't handle non-finite values.
Results may differ from the reference program's by a relative error of at most 0.0049.
Values may be sent and summed in bfloat16 or wider, within the bound.
A program may use at most 128 MiB of HBM per device.

```python
import jax
import jax.numpy as jnp
from jax import lax

F = 256
BLOCK = 128
MOST = 1
NB_DEV = 8
TILES_DEV = 128
NODES = 32768
N_ROW = 32
N_REP = 8


def tile_pairs(key):
    keys = jax.random.split(key, N_ROW * N_REP)
    picks = jax.vmap(lambda k: jax.random.permutation(k, N_ROW * NB_DEV)[:TILES_DEV])(keys)
    return picks.reshape(N_ROW, N_REP, TILES_DEV).astype(jnp.int32)


def draw_tile_source(key, part):
    pairs = tile_pairs(key)
    return (pairs // NB_DEV).astype(jnp.int32)


def draw_tile_target(key, part):
    pairs = tile_pairs(key)
    return (pairs % NB_DEV).astype(jnp.int32)


def draw_tiles(key, part):
    key = jax.random.fold_in(key, 23)
    spread = (6.0 * NB_DEV / (BLOCK * TILES_DEV * N_REP)) ** 0.5
    values = jax.random.uniform(key, (N_ROW, N_REP, TILES_DEV, BLOCK, BLOCK), jnp.float32, 0.0, spread)
    return values.astype(jnp.bfloat16)


def draw_live_tiles(key, part):
    key = jax.random.fold_in(key, 11)
    power = jax.random.randint(key, (N_ROW, N_REP), 0, 4)
    counts = jnp.maximum(1, TILES_DEV // jnp.power(2, power))
    counts = counts.at[0, 0].set(TILES_DEV)
    return counts.astype(jnp.int32)


def set_ends(values, stream_key, smallest, high):
    longest = values.shape.index(max(values.shape))
    spots = []
    for shift in (0, 1):
        where = [jax.random.randint(jax.random.fold_in(stream_key, axis), (), 0, length) for axis, length in enumerate(values.shape)]
        where[longest] = (where[longest] + shift) % values.shape[longest]
        spots.append(tuple(where))
    return values.at[spots[0]].set(smallest).at[spots[1]].set(high)


def steps_of(rng, extent, pieces, least, top_value):
    level = 1.0
    for position, blocks in pieces:
        draws = jax.random.uniform(jax.random.fold_in(jax.random.fold_in(rng, 6), position), (blocks,), jnp.float32, least / len(pieces), top_value / len(pieces))
        level = level * jnp.repeat(jnp.exp(draws), extent[position] // blocks).reshape((-1,) + (1,) * (len(extent) - 1 - position))
    return level


def bell_draw(stream_key, dims, width, bound, shards=(), kind=jnp.bfloat16):
    drawn = jax.random.normal(stream_key, dims, jnp.float32) * width
    if len(shards) > 0:
        drawn = steps_of(stream_key, dims, shards, -0.22, 0.18) * drawn
    return jnp.clip(drawn, min=-bound, max=bound).astype(kind)


def setup_inputs(seed: int = 0) -> dict:
    streams_of = jax.random.split(jax.random.key(seed), 8)
    return {
        "features": bell_draw(streams_of[0], (NODES, F), 1.0, 6.0, ((0, 256),)),
        "weight": bell_draw(streams_of[1], (F, F), F ** -0.5, 0.375),
        "tiles": draw_tiles(jax.random.fold_in(streams_of[7], 71), 0),
        "tile_source": draw_tile_source(jax.random.fold_in(streams_of[7], 71), 0),
        "tile_target": draw_tile_target(jax.random.fold_in(streams_of[7], 71), 0),
        "live_tiles": draw_live_tiles(jax.random.fold_in(streams_of[7], 71), 0),
        "wanted": set_ends(jax.random.randint(streams_of[6], (N_ROW, N_REP, N_ROW, MOST), 0, NB_DEV), jax.random.fold_in(streams_of[6], 1), 0, NB_DEV - 1).astype(jnp.int32),
    }


def reference(features, weight, tiles, tile_source, tile_target, live_tiles, wanted):
    hidden = jnp.dot(features, weight, preferred_element_type=jnp.float32).astype(jnp.bfloat16)
    blocks = hidden.reshape(N_ROW * NB_DEV, BLOCK, F)
    starts = (jnp.arange(N_ROW, dtype=jnp.int32) * NB_DEV)[:, None]
    slots = jnp.arange(TILES_DEV, dtype=jnp.int32)
    targets = jnp.arange(NB_DEV, dtype=jnp.int32)

    def one_slab(r):
        total = jnp.zeros((NB_DEV, BLOCK, F), jnp.float32)
        for q in range(N_REP):
            index = (starts + wanted[r, q]).reshape(-1).astype(jnp.int32)
            panels = blocks[index]
            chosen = panels[tile_source[r, q]]
            products = jnp.einsum("tij,tjf->tif", tiles[r, q].astype(jnp.float32), chosen.astype(jnp.float32))
            alive = (slots < live_tiles[r, q]).astype(jnp.float32)
            onehot = (tile_target[r, q][None, :] == targets[:, None]).astype(jnp.float32) * alive[None, :]
            total = total + jnp.einsum("bt,tif->bif", onehot, products, precision=lax.Precision.HIGHEST)
        return total

    result = lax.map(one_slab, jnp.arange(N_ROW, dtype=jnp.int32))
    return result.reshape(NODES, F).astype(jnp.bfloat16)
```

```python
import functools

import jax
import jax.numpy as jnp
from jax import lax
from jax.experimental import pallas as pl
from jax.experimental.pallas import tpu as pltpu
from jax.sharding import PartitionSpec as P

F = 256
BLOCK = 128
NB = 8
TILES = 128
SLABS = 32
GROUP = 4
MESH = pl.DeviceIdType.MESH

OFFSETS = [
    (2, 0, 0), (0, 2, 0), (1, 1, 0), (3, 3, 0),
    (1, 3, 0), (3, 1, 0), (1, 0, 1), (3, 0, 1),
    (0, 1, 1), (0, 3, 1), (0, 0, 1), (1, 0, 0),
    (3, 0, 0), (0, 1, 0), (0, 3, 0), (0, 0, 0),
]
HOME = OFFSETS.index((0, 0, 0))
N_OFF = len(OFFSETS)


def device(x, y, z, c):
    return (z * 4 + (y // 2) * 2 + c, lax.rem(y, 2) * 4 + x)


def owned_slab(x, y, z, c):
    odd = lax.rem(z, 2)
    zs = lax.rem(x + 2 * odd, 4) + 4 * lax.rem(y, 2)
    yh = lax.rem(y // 2 + odd + lax.rem(zs, 2) + 1, 2)
    return zs, yh


def owner_at(zs, yh, c, z):
    odd = lax.rem(z, 2)
    x = lax.rem(lax.rem(zs, 4) + 2 * odd, 4)
    pair = lax.rem(yh + odd + lax.rem(zs, 2) + 1, 2)
    return device(x, 2 * pair + zs // 4, z, c)


def kernel(
    live_ref, features_ref, weight_ref, tiles_ref, source_ref, target_ref, wanted_ref, out_ref,
    feat_v, weight_v, hidden_v, tiles_v, dense_v, slab_v, picked_v, panel_v, total_v, part_v, land_v,
    ask_v, req_v, slot_v, req_s, slot_s,
    load_sem, small_sem, spread_send, spread_recv, ask_send, ask_recv, give_send, give_recv, sum_send, sum_recv,
):
    r, q = lax.axis_index("row"), lax.axis_index("rep")
    z, yh, c = r // 4, lax.rem(r // 2, 2), lax.rem(r, 2)
    yl, x = q // 4, lax.rem(q, 4)
    y = yh * 2 + yl

    loads = [
        pltpu.make_async_copy(features_ref, feat_v, load_sem.at[0]),
        pltpu.make_async_copy(weight_ref, weight_v, load_sem.at[1]),
        pltpu.make_async_copy(tiles_ref.at[0, 0], tiles_v.at[pl.ds(0, TILES)], load_sem.at[2]),
    ]
    for load in loads:
        load.start()

    def owner_of(k, core):
        dx, dy, dz = OFFSETS[k]
        pz = lax.rem(z + dz * (1 - 2 * core) + 8, 8) if dz else z
        return lax.rem(x + dx, 4), lax.rem(y + dy, 4), pz, core

    def asker_of(k, core):
        dx, dy, dz = OFFSETS[k]
        pz = lax.rem(z - dz * (1 - 2 * c) + 8, 8) if dz else z
        return lax.rem(x + 4 - dx, 4), lax.rem(y + 4 - dy, 4), pz, core

    own_z, own_yh = owned_slab(x, y, z, c)
    own = own_z * 4 + own_yh * 2 + c

    barrier = pltpu.get_barrier_semaphore()
    n_signals = 0

    def tell(dev):
        pl.semaphore_signal(barrier, inc=1, device_id=dev, device_id_type=MESH)

    for b in range(NB):
        tell(device(b % 4, 2 * own_yh + b // 4, own_z, c))
    n_signals += NB
    for k in range(N_OFF):
        cores = (1 - c,) if k == HOME else (0, 1)
        for core in cores:
            tell(device(*owner_of(k, core)))
            tell(device(*asker_of(k, core)))
        n_signals += 2 * len(cores)
    for d in range(1, NB):
        tell((r, lax.rem(q + d, NB)))
    n_signals += NB - 1

    loads[0].wait()
    loads[1].wait()
    hidden_v[...] = jnp.dot(feat_v[...], weight_v[...], preferred_element_type=jnp.float32).astype(jnp.bfloat16)
    ask_v[...] = jnp.zeros_like(ask_v)
    ask_v[:, 0:SLABS] = wanted_ref[...]

    pl.semaphore_wait(barrier, n_signals)

    spreads = []
    for dz in (4, 3, 5, 2, 6, 1, 7, 0):
        spread = pltpu.make_async_remote_copy(
            src_ref=hidden_v, dst_ref=slab_v.at[q], send_sem=spread_send.at[dz], recv_sem=spread_recv.at[q],
            device_id=owner_at(z, yh, c, lax.rem(z + dz, 8)), device_id_type=MESH,
        )
        spread.start()
        spreads.append(spread)
    asks = []
    for k in range(N_OFF):
        for core in (1 - c,) if k == HOME else (0, 1):
            ask = pltpu.make_async_remote_copy(
                src_ref=ask_v, dst_ref=req_v.at[2 * k + c], send_sem=ask_send.at[2 * k + core],
                recv_sem=ask_recv.at[2 * k + c], device_id=device(*owner_of(k, core)), device_id_type=MESH,
            )
            ask.start()
            asks.append(ask)
    mine = pltpu.make_async_copy(ask_v, req_v.at[2 * HOME + c], small_sem.at[0])
    mine.start()

    t_row = lax.broadcasted_iota(jnp.int32, (1, TILES), 1)
    key = jnp.where(t_row < live_ref[0, 0], target_ref[...] * SLABS + source_ref[...], -1)
    here = lax.broadcasted_iota(jnp.int32, (TILES, TILES), 0) == lax.broadcasted_iota(jnp.int32, (TILES, TILES), 1)
    column = jnp.sum(jnp.where(here, jnp.broadcast_to(key, (TILES, TILES)), 0), axis=1, keepdims=True)
    pair = lax.broadcasted_iota(jnp.int32, (TILES, NB * SLABS), 1)
    slot = lax.broadcasted_iota(jnp.int32, (TILES, NB * SLABS), 0)
    found = jnp.where(jnp.broadcast_to(column, (TILES, NB * SLABS)) == pair, slot - TILES, 0)
    slot_v[...] = jnp.sum(found, axis=0, keepdims=True) + TILES
    to_scalar = pltpu.make_async_copy(slot_v, slot_s, small_sem.at[1])
    to_scalar.start()
    tiles_v[TILES] = jnp.zeros((BLOCK, BLOCK), jnp.bfloat16)
    loads[2].wait()
    to_scalar.wait()

    def place(k):
        for core in (0, 1):
            px, py, pz, _ = owner_of(k, core)
            sz, syh = owned_slab(px, py, pz, core)
            s = sz * 4 + syh * 2 + core
            for b in range(NB):
                t = slot_s[0, b * SLABS + s]
                at = (k % GROUP) * 2 * BLOCK + core * BLOCK
                dense_v[k // GROUP, b * BLOCK : (b + 1) * BLOCK, at : at + BLOCK] = tiles_v[t]

    for k in range(N_OFF):
        place(k)

    mine.wait()
    for k in range(N_OFF):
        for core in (1 - c,) if k == HOME else (0, 1):
            pltpu.make_async_remote_copy(
                src_ref=ask_v, dst_ref=req_v.at[2 * k + core], send_sem=ask_send.at[2 * k + core],
                recv_sem=ask_recv.at[2 * k + core], device_id=device(*asker_of(k, core)), device_id_type=MESH,
            ).wait_recv()
    to_scalar = pltpu.make_async_copy(req_v, req_s, small_sem.at[2])
    to_scalar.start()
    to_scalar.wait()

    for b in range(NB):
        pltpu.make_async_remote_copy(
            src_ref=hidden_v, dst_ref=slab_v.at[b], send_sem=spread_send.at[b], recv_sem=spread_recv.at[b],
            device_id=device(b % 4, 2 * own_yh + b // 4, own_z, c), device_id_type=MESH,
        ).wait_recv()

    gives = []
    for k in range(N_OFF):
        for core in (1 - c,) if k == HOME else (0, 1):
            index = 2 * k + core
            picked_v[index] = slab_v[req_s[index, 0, own]]
            give = pltpu.make_async_remote_copy(
                src_ref=picked_v.at[index], dst_ref=panel_v.at[k, c], send_sem=give_send.at[index],
                recv_sem=give_recv.at[2 * k + c], device_id=device(*asker_of(k, core)), device_id_type=MESH,
            )
            give.start()
            gives.append(give)
    panel_v[HOME, c] = slab_v[req_s[2 * HOME + c, 0, own]]

    def arrive(g):
        for k in range(g * GROUP, (g + 1) * GROUP):
            for core in (1 - c,) if k == HOME else (0, 1):
                pltpu.make_async_remote_copy(
                    src_ref=picked_v.at[0], dst_ref=panel_v.at[k, core], send_sem=give_send.at[2 * k + core],
                    recv_sem=give_recv.at[2 * k + core], device_id=device(*owner_of(k, core)), device_id_type=MESH,
                ).wait_recv()

    def panels(g):
        return panel_v[g * GROUP : (g + 1) * GROUP].reshape(2 * GROUP * BLOCK, F)

    ROWS = 256
    last = N_OFF // GROUP - 1
    for g in range(last):
        arrive(g)

        @pl.loop(0, NB * BLOCK // ROWS)
        def _(i):
            at = pl.ds(pl.multiple_of(i * ROWS, ROWS), ROWS)
            term = jnp.dot(dense_v[g, at, :], panels(g), preferred_element_type=jnp.float32)
            if g == 0:
                total_v[at, :] = term
            else:
                total_v[at, :] += term

    arrive(last)
    sums = []
    for d in range(1, NB + 1):
        b = lax.rem(q + d, NB)
        at = pl.ds(pl.multiple_of(b * BLOCK, BLOCK), BLOCK)
        full = total_v[at, :] + jnp.dot(dense_v[last, at, :], panels(last), preferred_element_type=jnp.float32)
        if d < NB:
            part_v[d] = full.astype(jnp.bfloat16)
            part = pltpu.make_async_remote_copy(
                src_ref=part_v.at[d], dst_ref=land_v.at[d], send_sem=sum_send.at[d], recv_sem=sum_recv.at[d],
                device_id=(r, b), device_id_type=MESH,
            )
            part.start()
            sums.append(part)
        else:
            total_v[0:BLOCK, :] = full
    for part in sums:
        part.wait_recv()
    result = total_v[0:BLOCK, :]
    for d in range(1, NB):
        result += land_v[d].astype(jnp.float32)
    out_ref[...] = result.astype(jnp.bfloat16)
    for copy in spreads + asks + gives + sums:
        copy.wait_send()


def local(features, weight, tiles, tile_source, tile_target, live_tiles, wanted):
    vmem = pl.BlockSpec(memory_space=pltpu.VMEM)
    hbm = pl.BlockSpec(memory_space=pl.ANY)
    smem = pl.BlockSpec(memory_space=pltpu.SMEM)
    dma = pltpu.SemaphoreType.DMA
    bf16, f32, i32 = jnp.bfloat16, jnp.float32, jnp.int32
    return pl.pallas_call(
        kernel,
        out_shape=jax.ShapeDtypeStruct((BLOCK, F), bf16),
        in_specs=[smem, hbm, hbm, hbm, vmem, vmem, vmem],
        out_specs=vmem,
        scratch_shapes=[
            pltpu.VMEM((BLOCK, F), bf16),
            pltpu.VMEM((F, F), bf16),
            pltpu.VMEM((BLOCK, F), bf16),
            pltpu.VMEM((TILES + 1, BLOCK, BLOCK), bf16),
            pltpu.VMEM((N_OFF // GROUP, NB * BLOCK, 2 * GROUP * BLOCK), bf16),
            pltpu.VMEM((NB, BLOCK, F), bf16),
            pltpu.VMEM((2 * N_OFF, BLOCK, F), bf16),
            pltpu.VMEM((N_OFF, 2, BLOCK, F), bf16),
            pltpu.VMEM((NB * BLOCK, F), f32),
            pltpu.VMEM((NB, BLOCK, F), bf16),
            pltpu.VMEM((NB, BLOCK, F), bf16),
            pltpu.VMEM((1, 128), i32),
            pltpu.VMEM((2 * N_OFF, 1, 128), i32),
            pltpu.VMEM((1, NB * SLABS), i32),
            pltpu.SMEM((2 * N_OFF, 1, 128), i32),
            pltpu.SMEM((1, NB * SLABS), i32),
            dma((3,)), dma((3,)),
            dma((NB,)), dma((NB,)),
            dma((2 * N_OFF,)), dma((2 * N_OFF,)),
            dma((2 * N_OFF,)), dma((2 * N_OFF,)),
            dma((NB,)), dma((NB,)),
        ],
        compiler_params=pltpu.CompilerParams(
            collective_id=0, has_side_effects=True, vmem_limit_bytes=48 << 20
        ),
    )(
        live_tiles, features, weight, tiles,
        tile_source.reshape(1, TILES), tile_target.reshape(1, TILES), wanted.reshape(1, SLABS),
    )


def solution(mesh):
    placed = (
        P(("row", "rep"), None),
        P(),
        P("row", "rep", None, None, None),
        P("row", "rep", None),
        P("row", "rep", None),
        P("row", "rep"),
        P("row", "rep", None, None),
    )
    return jax.shard_map(
        local, mesh=mesh, in_specs=placed, out_specs=P(("row", "rep"), None), check_vma=False
    )
```

```python
import functools

import jax
import jax.numpy as jnp
from jax import lax
from jax.experimental import pallas as pl
from jax.experimental.pallas import tpu as pltpu
from jax.sharding import PartitionSpec as P

F = 256
BLOCK = 128
NB = 8
TILES = 128
SLABS = 32
GROUP = 4
MESH = pl.DeviceIdType.MESH

OFFSETS = [
    (2, 0, 0), (0, 2, 0), (1, 1, 0), (3, 3, 0),
    (1, 3, 0), (3, 1, 0), (1, 0, 1), (3, 0, 1),
    (0, 1, 1), (0, 3, 1), (0, 0, 1), (1, 0, 0),
    (3, 0, 0), (0, 1, 0), (0, 3, 0), (0, 0, 0),
]
HOME = OFFSETS.index((0, 0, 0))
N_OFF = len(OFFSETS)


def device(x, y, z, c):
    return (z * 4 + (y // 2) * 2 + c, lax.rem(y, 2) * 4 + x)


def owned_slab(x, y, z, c):
    odd = lax.rem(z, 2)
    zs = lax.rem(x + 2 * odd, 4) + 4 * lax.rem(y, 2)
    yh = lax.rem(y // 2 + odd + lax.rem(zs, 2) + 1, 2)
    return zs, yh


def owner_at(zs, yh, c, z):
    odd = lax.rem(z, 2)
    x = lax.rem(lax.rem(zs, 4) + 2 * odd, 4)
    pair = lax.rem(yh + odd + lax.rem(zs, 2) + 1, 2)
    return device(x, 2 * pair + zs // 4, z, c)


def kernel(
    live_ref, features_ref, weight_ref, tiles_ref, source_ref, target_ref, wanted_ref, out_ref,
    feat_v, weight_v, hidden_v, tiles_v, dense_v, slab_v, picked_v, panel_v, total_v, part_v, land_v,
    source_v, target_v, wanted_v, ask_v, req_v, slot_v, req_s, slot_s,
    load_sem, small_sem, spread_send, spread_recv, ask_send, ask_recv, give_send, give_recv, sum_send, sum_recv,
):
    r, q = lax.axis_index("row"), lax.axis_index("rep")
    z, yh, c = r // 4, lax.rem(r // 2, 2), lax.rem(r, 2)
    yl, x = q // 4, lax.rem(q, 4)
    y = yh * 2 + yl

    loads = [
        pltpu.make_async_copy(features_ref, feat_v, load_sem.at[0]),
        pltpu.make_async_copy(weight_ref, weight_v, load_sem.at[1]),
        pltpu.make_async_copy(wanted_ref, wanted_v, load_sem.at[2]),
        pltpu.make_async_copy(source_ref, source_v, load_sem.at[3]),
        pltpu.make_async_copy(target_ref, target_v, load_sem.at[4]),
        pltpu.make_async_copy(tiles_ref.at[0, 0], tiles_v.at[pl.ds(0, TILES)], load_sem.at[5]),
    ]
    for load in loads:
        load.start()

    def owner_of(k, core):
        dx, dy, dz = OFFSETS[k]
        pz = lax.rem(z + dz * (1 - 2 * core) + 8, 8) if dz else z
        return lax.rem(x + dx, 4), lax.rem(y + dy, 4), pz, core

    def asker_of(k, core):
        dx, dy, dz = OFFSETS[k]
        pz = lax.rem(z - dz * (1 - 2 * c) + 8, 8) if dz else z
        return lax.rem(x + 4 - dx, 4), lax.rem(y + 4 - dy, 4), pz, core

    own_z, own_yh = owned_slab(x, y, z, c)
    own = own_z * 4 + own_yh * 2 + c

    barrier = pltpu.get_barrier_semaphore()
    n_signals = 0

    def tell(dev):
        pl.semaphore_signal(barrier, inc=1, device_id=dev, device_id_type=MESH)

    for b in range(NB):
        tell(device(b % 4, 2 * own_yh + b // 4, own_z, c))
    n_signals += NB
    for k in range(N_OFF):
        cores = (1 - c,) if k == HOME else (0, 1)
        for core in cores:
            tell(device(*asker_of(k, core)))
        n_signals += len(cores)

    loads[0].wait()
    loads[1].wait()
    hidden_v[...] = jnp.dot(feat_v[...], weight_v[...], preferred_element_type=jnp.float32).astype(jnp.bfloat16)
    ask_v[...] = jnp.zeros_like(ask_v)
    loads[2].wait()
    ask_v[:, 0:SLABS] = wanted_v[...]

    pl.semaphore_wait(barrier, n_signals)

    spreads = []
    for dz in (0, 1, 7, 2, 6, 3, 5, 4):
        spread = pltpu.make_async_remote_copy(
            src_ref=hidden_v, dst_ref=slab_v.at[q], send_sem=spread_send.at[dz], recv_sem=spread_recv.at[q],
            device_id=owner_at(z, yh, c, lax.rem(z + dz, 8)), device_id_type=MESH,
        )
        spread.start()
        spreads.append(spread)
    asks = []
    for k in range(N_OFF):
        for core in (1 - c,) if k == HOME else (0, 1):
            ask = pltpu.make_async_remote_copy(
                src_ref=ask_v, dst_ref=req_v.at[2 * k + c], send_sem=ask_send.at[2 * k + core],
                recv_sem=ask_recv.at[2 * k + c], device_id=device(*owner_of(k, core)), device_id_type=MESH,
            )
            ask.start()
            asks.append(ask)
    mine = pltpu.make_async_copy(ask_v, req_v.at[2 * HOME + c], small_sem.at[0])
    mine.start()

    loads[3].wait()
    loads[4].wait()
    t_row = lax.broadcasted_iota(jnp.int32, (1, TILES), 1)
    key = jnp.where(t_row < live_ref[0, 0], target_v[...] * SLABS + source_v[...], -1)
    here = lax.broadcasted_iota(jnp.int32, (TILES, TILES), 0) == lax.broadcasted_iota(jnp.int32, (TILES, TILES), 1)
    column = jnp.sum(jnp.where(here, jnp.broadcast_to(key, (TILES, TILES)), 0), axis=1, keepdims=True)
    pair = lax.broadcasted_iota(jnp.int32, (TILES, NB * SLABS), 1)
    slot = lax.broadcasted_iota(jnp.int32, (TILES, NB * SLABS), 0)
    found = jnp.where(jnp.broadcast_to(column, (TILES, NB * SLABS)) == pair, slot - TILES, 0)
    slot_v[...] = jnp.sum(found, axis=0, keepdims=True) + TILES
    to_scalar = pltpu.make_async_copy(slot_v, slot_s, small_sem.at[1])
    to_scalar.start()
    tiles_v[TILES] = jnp.zeros((BLOCK, BLOCK), jnp.bfloat16)
    loads[5].wait()
    to_scalar.wait()

    def place(k):
        for core in (0, 1):
            px, py, pz, _ = owner_of(k, core)
            sz, syh = owned_slab(px, py, pz, core)
            s = sz * 4 + syh * 2 + core
            for b in range(NB):
                t = slot_s[0, b * SLABS + s]
                at = (k % GROUP) * 2 * BLOCK + core * BLOCK
                dense_v[k // GROUP, b * BLOCK : (b + 1) * BLOCK, at : at + BLOCK] = tiles_v[t]

    for k in range(N_OFF):
        place(k)

    mine.wait()
    for k in range(N_OFF):
        for core in (1 - c,) if k == HOME else (0, 1):
            pltpu.make_async_remote_copy(
                src_ref=ask_v, dst_ref=req_v.at[2 * k + core], send_sem=ask_send.at[2 * k + core],
                recv_sem=ask_recv.at[2 * k + core], device_id=device(*asker_of(k, core)), device_id_type=MESH,
            ).wait_recv()
    to_scalar = pltpu.make_async_copy(req_v, req_s, small_sem.at[2])
    to_scalar.start()
    to_scalar.wait()

    for b in range(NB):
        pltpu.make_async_remote_copy(
            src_ref=hidden_v, dst_ref=slab_v.at[b], send_sem=spread_send.at[b], recv_sem=spread_recv.at[b],
            device_id=device(b % 4, 2 * own_yh + b // 4, own_z, c), device_id_type=MESH,
        ).wait_recv()

    gives = []
    for k in range(N_OFF):
        for core in (1 - c,) if k == HOME else (0, 1):
            index = 2 * k + core
            picked_v[index] = slab_v[req_s[index, 0, own]]
            give = pltpu.make_async_remote_copy(
                src_ref=picked_v.at[index], dst_ref=panel_v.at[k, c], send_sem=give_send.at[index],
                recv_sem=give_recv.at[2 * k + c], device_id=device(*asker_of(k, core)), device_id_type=MESH,
            )
            give.start()
            gives.append(give)
    panel_v[HOME, c] = slab_v[req_s[2 * HOME + c, 0, own]]

    def arrive(g):
        for k in range(g * GROUP, (g + 1) * GROUP):
            for core in (1 - c,) if k == HOME else (0, 1):
                pltpu.make_async_remote_copy(
                    src_ref=picked_v.at[0], dst_ref=panel_v.at[k, core], send_sem=give_send.at[2 * k + core],
                    recv_sem=give_recv.at[2 * k + core], device_id=device(*owner_of(k, core)), device_id_type=MESH,
                ).wait_recv()

    def panels(g):
        return panel_v[g * GROUP : (g + 1) * GROUP].reshape(2 * GROUP * BLOCK, F)

    ROWS = 256
    last = N_OFF // GROUP - 1
    for g in range(last):
        arrive(g)

        @pl.loop(0, NB * BLOCK // ROWS)
        def _(i):
            at = pl.ds(pl.multiple_of(i * ROWS, ROWS), ROWS)
            term = jnp.dot(dense_v[g, at, :], panels(g), preferred_element_type=jnp.float32)
            if g == 0:
                total_v[at, :] = term
            else:
                total_v[at, :] += term

    arrive(last)
    sums = []
    for d in range(1, NB + 1):
        b = lax.rem(q + d, NB)
        at = pl.ds(pl.multiple_of(b * BLOCK, BLOCK), BLOCK)
        full = total_v[at, :] + jnp.dot(dense_v[last, at, :], panels(last), preferred_element_type=jnp.float32)
        if d < NB:
            part_v[d] = full.astype(jnp.bfloat16)
            part = pltpu.make_async_remote_copy(
                src_ref=part_v.at[d], dst_ref=land_v.at[d], send_sem=sum_send.at[d], recv_sem=sum_recv.at[d],
                device_id=(r, b), device_id_type=MESH,
            )
            part.start()
            sums.append(part)
        else:
            total_v[0:BLOCK, :] = full
    for part in sums:
        part.wait_recv()
    result = total_v[0:BLOCK, :]
    for d in range(1, NB):
        result += land_v[d].astype(jnp.float32)
    out_ref[...] = result.astype(jnp.bfloat16)
    for copy in spreads + asks + gives + sums:
        copy.wait_send()


def local(features, weight, tiles, tile_source, tile_target, live_tiles, wanted):
    vmem = pl.BlockSpec(memory_space=pltpu.VMEM)
    hbm = pl.BlockSpec(memory_space=pl.ANY)
    smem = pl.BlockSpec(memory_space=pltpu.SMEM)
    dma = pltpu.SemaphoreType.DMA
    bf16, f32, i32 = jnp.bfloat16, jnp.float32, jnp.int32
    return pl.pallas_call(
        kernel,
        out_shape=jax.ShapeDtypeStruct((BLOCK, F), bf16),
        in_specs=[smem, hbm, hbm, hbm, hbm, hbm, hbm],
        out_specs=vmem,
        scratch_shapes=[
            pltpu.VMEM((BLOCK, F), bf16),
            pltpu.VMEM((F, F), bf16),
            pltpu.VMEM((BLOCK, F), bf16),
            pltpu.VMEM((TILES + 1, BLOCK, BLOCK), bf16),
            pltpu.VMEM((N_OFF // GROUP, NB * BLOCK, 2 * GROUP * BLOCK), bf16),
            pltpu.VMEM((NB, BLOCK, F), bf16),
            pltpu.VMEM((2 * N_OFF, BLOCK, F), bf16),
            pltpu.VMEM((N_OFF, 2, BLOCK, F), bf16),
            pltpu.VMEM((NB * BLOCK, F), f32),
            pltpu.VMEM((NB, BLOCK, F), bf16),
            pltpu.VMEM((NB, BLOCK, F), bf16),
            pltpu.VMEM((1, TILES), i32),
            pltpu.VMEM((1, TILES), i32),
            pltpu.VMEM((1, SLABS), i32),
            pltpu.VMEM((1, 128), i32),
            pltpu.VMEM((2 * N_OFF, 1, 128), i32),
            pltpu.VMEM((1, NB * SLABS), i32),
            pltpu.SMEM((2 * N_OFF, 1, 128), i32),
            pltpu.SMEM((1, NB * SLABS), i32),
            dma((6,)), dma((3,)),
            dma((NB,)), dma((NB,)),
            dma((2 * N_OFF,)), dma((2 * N_OFF,)),
            dma((2 * N_OFF,)), dma((2 * N_OFF,)),
            dma((NB,)), dma((NB,)),
        ],
        compiler_params=pltpu.CompilerParams(
            collective_id=0, has_side_effects=True, vmem_limit_bytes=63 << 20
        ),
    )(
        live_tiles, features, weight, tiles,
        tile_source.reshape(1, TILES), tile_target.reshape(1, TILES), wanted.reshape(1, SLABS),
    )


def solution(mesh):
    placed = (
        P(("row", "rep"), None),
        P(),
        P("row", "rep", None, None, None),
        P("row", "rep", None),
        P("row", "rep", None),
        P("row", "rep"),
        P("row", "rep", None, None),
    )
    return jax.shard_map(
        local, mesh=mesh, in_specs=placed, out_specs=P(("row", "rep"), None), check_vma=False
    )
```

```python
import functools

import jax
import jax.numpy as jnp
from jax import lax
from jax.experimental import pallas as pl
from jax.experimental.pallas import tpu as pltpu
from jax.sharding import PartitionSpec as P

F = 256
BLOCK = 128
NB = 8
TILES = 128
SLABS = 32
GROUP = 4
MESH = pl.DeviceIdType.MESH

OFFSETS = [
    (2, 0, 0), (0, 2, 0), (1, 1, 0), (3, 3, 0),
    (1, 3, 0), (3, 1, 0), (1, 0, 1), (3, 0, 1),
    (0, 1, 1), (0, 3, 1), (0, 0, 1), (1, 0, 0),
    (3, 0, 0), (0, 1, 0), (0, 3, 0), (0, 0, 0),
]
HOME = OFFSETS.index((0, 0, 0))
N_OFF = len(OFFSETS)
PARTS = 2
WIDE = F // PARTS


def device(x, y, z, c):
    return (z * 4 + (y // 2) * 2 + c, lax.rem(y, 2) * 4 + x)


def owned_slab(x, y, z, c):
    odd = lax.rem(z, 2)
    zs = lax.rem(x + 2 * odd, 4) + 4 * lax.rem(y, 2)
    yh = lax.rem(y // 2 + odd + lax.rem(zs, 2) + 1, 2)
    return zs, yh


def owner_at(zs, yh, c, z):
    odd = lax.rem(z, 2)
    x = lax.rem(lax.rem(zs, 4) + 2 * odd, 4)
    pair = lax.rem(yh + odd + lax.rem(zs, 2) + 1, 2)
    return device(x, 2 * pair + zs // 4, z, c)


def kernel(
    live_ref, features_ref, weight_ref, tiles_ref, source_ref, target_ref, wanted_ref, out_ref,
    feat_v, weight_v, hidden_v, tiles_v, dense_v, slab_0_v, slab_1_v, picked_v, panel_v, total_v, rest_v, part_v, land_v,
    source_v, target_v, wanted_v, ask_v, req_v, slot_v, req_s, slot_s,
    load_sem, small_sem, spread_send, spread_recv, ask_send, ask_recv, give_send, give_recv, sum_send, sum_recv,
):
    slabs_v = (slab_0_v, slab_1_v)
    r, q = lax.axis_index("row"), lax.axis_index("rep")
    z, yh, c = r // 4, lax.rem(r // 2, 2), lax.rem(r, 2)
    yl, x = q // 4, lax.rem(q, 4)
    y = yh * 2 + yl

    loads = [
        pltpu.make_async_copy(features_ref, feat_v, load_sem.at[0]),
        pltpu.make_async_copy(weight_ref, weight_v, load_sem.at[1]),
        pltpu.make_async_copy(wanted_ref, wanted_v, load_sem.at[2]),
        pltpu.make_async_copy(source_ref, source_v, load_sem.at[3]),
        pltpu.make_async_copy(target_ref, target_v, load_sem.at[4]),
        pltpu.make_async_copy(tiles_ref.at[0, 0], tiles_v.at[pl.ds(0, TILES)], load_sem.at[5]),
    ]
    for load in loads:
        load.start()

    def owner_of(k, core):
        dx, dy, dz = OFFSETS[k]
        pz = lax.rem(z + dz * (1 - 2 * core) + 8, 8) if dz else z
        return lax.rem(x + dx, 4), lax.rem(y + dy, 4), pz, core

    def asker_of(k, core):
        dx, dy, dz = OFFSETS[k]
        pz = lax.rem(z - dz * (1 - 2 * c) + 8, 8) if dz else z
        return lax.rem(x + 4 - dx, 4), lax.rem(y + 4 - dy, 4), pz, core

    own_z, own_yh = owned_slab(x, y, z, c)
    own = own_z * 4 + own_yh * 2 + c

    barrier = pltpu.get_barrier_semaphore()
    n_signals = 0

    def tell(dev):
        pl.semaphore_signal(barrier, inc=1, device_id=dev, device_id_type=MESH)

    for b in range(NB):
        tell(device(b % 4, 2 * own_yh + b // 4, own_z, c))
    n_signals += NB
    for k in range(N_OFF):
        cores = (1 - c,) if k == HOME else (0, 1)
        for core in cores:
            tell(device(*asker_of(k, core)))
        n_signals += len(cores)

    loads[0].wait()
    loads[1].wait()
    hidden = jnp.dot(feat_v[...], weight_v[...], preferred_element_type=jnp.float32).astype(jnp.bfloat16)
    for h in range(PARTS):
        hidden_v[h] = hidden[:, h * WIDE : (h + 1) * WIDE]
    ask_v[...] = jnp.zeros_like(ask_v)
    loads[2].wait()
    ask_v[:, 0:SLABS] = wanted_v[...]

    pl.semaphore_wait(barrier, n_signals)

    spreads = []

    def spread_part(h):
        for dz in (0, 1, 7, 2, 6, 3, 5, 4):
            spread = pltpu.make_async_remote_copy(
                src_ref=hidden_v.at[h], dst_ref=slabs_v[h].at[q], send_sem=spread_send.at[h, dz], recv_sem=spread_recv.at[h, q],
                device_id=owner_at(z, yh, c, lax.rem(z + dz, 8)), device_id_type=MESH,
            )
            spread.start()
            spreads.append(spread)

    spread_part(0)
    asks = []
    for k in range(N_OFF):
        for core in (1 - c,) if k == HOME else (0, 1):
            ask = pltpu.make_async_remote_copy(
                src_ref=ask_v, dst_ref=req_v.at[2 * k + c], send_sem=ask_send.at[2 * k + core],
                recv_sem=ask_recv.at[2 * k + c], device_id=device(*owner_of(k, core)), device_id_type=MESH,
            )
            ask.start()
            asks.append(ask)
    for h in range(1, PARTS):
        spread_part(h)
    mine = pltpu.make_async_copy(ask_v, req_v.at[2 * HOME + c], small_sem.at[0])
    mine.start()

    loads[3].wait()
    loads[4].wait()
    t_row = lax.broadcasted_iota(jnp.int32, (1, TILES), 1)
    key = jnp.where(t_row < live_ref[0, 0], target_v[...] * SLABS + source_v[...], -1)
    here = lax.broadcasted_iota(jnp.int32, (TILES, TILES), 0) == lax.broadcasted_iota(jnp.int32, (TILES, TILES), 1)
    column = jnp.sum(jnp.where(here, jnp.broadcast_to(key, (TILES, TILES)), 0), axis=1, keepdims=True)
    pair = lax.broadcasted_iota(jnp.int32, (TILES, NB * SLABS), 1)
    slot = lax.broadcasted_iota(jnp.int32, (TILES, NB * SLABS), 0)
    found = jnp.where(jnp.broadcast_to(column, (TILES, NB * SLABS)) == pair, slot - TILES, 0)
    slot_v[...] = jnp.sum(found, axis=0, keepdims=True) + TILES
    to_scalar = pltpu.make_async_copy(slot_v, slot_s, small_sem.at[1])
    to_scalar.start()
    tiles_v[TILES] = jnp.zeros((BLOCK, BLOCK), jnp.bfloat16)
    loads[5].wait()
    to_scalar.wait()

    def place(k):
        for core in (0, 1):
            px, py, pz, _ = owner_of(k, core)
            sz, syh = owned_slab(px, py, pz, core)
            s = sz * 4 + syh * 2 + core
            at = (k % GROUP) * 2 * BLOCK + core * BLOCK

            @pl.loop(0, NB)
            def _(b):
                rows = pl.ds(pl.multiple_of(b * BLOCK, BLOCK), BLOCK)
                dense_v[k // GROUP, rows, at : at + BLOCK] = tiles_v[slot_s[0, b * SLABS + s]]

    for k in range(N_OFF):
        place(k)

    mine.wait()
    for k in range(N_OFF):
        for core in (1 - c,) if k == HOME else (0, 1):
            pltpu.make_async_remote_copy(
                src_ref=ask_v, dst_ref=req_v.at[2 * k + core], send_sem=ask_send.at[2 * k + core],
                recv_sem=ask_recv.at[2 * k + core], device_id=device(*asker_of(k, core)), device_id_type=MESH,
            ).wait_recv()
    to_scalar = pltpu.make_async_copy(req_v, req_s, small_sem.at[2])
    to_scalar.start()
    to_scalar.wait()

    gives = []
    for h in range(PARTS):
        for b in range(NB):
            pltpu.make_async_remote_copy(
                src_ref=hidden_v.at[h], dst_ref=slabs_v[h].at[b], send_sem=spread_send.at[h, b], recv_sem=spread_recv.at[h, b],
                device_id=device(b % 4, 2 * own_yh + b // 4, own_z, c), device_id_type=MESH,
            ).wait_recv()
        for k in range(N_OFF):
            for core in (1 - c,) if k == HOME else (0, 1):
                index = 2 * k + core
                picked_v[h, index] = slabs_v[h][req_s[index, 0, own]]
                give = pltpu.make_async_remote_copy(
                    src_ref=picked_v.at[h, index], dst_ref=panel_v.at[h, k, c], send_sem=give_send.at[h, index],
                    recv_sem=give_recv.at[h, 2 * k + c], device_id=device(*asker_of(k, core)), device_id_type=MESH,
                )
                give.start()
                gives.append(give)
        panel_v[h, HOME, c] = slabs_v[h][req_s[2 * HOME + c, 0, own]]

    def arrive(h, g):
        for k in range(g * GROUP, (g + 1) * GROUP):
            for core in (1 - c,) if k == HOME else (0, 1):
                pltpu.make_async_remote_copy(
                    src_ref=picked_v.at[h, 0], dst_ref=panel_v.at[h, k, core], send_sem=give_send.at[h, 2 * k + core],
                    recv_sem=give_recv.at[h, 2 * k + core], device_id=device(*owner_of(k, core)), device_id_type=MESH,
                ).wait_recv()

    def panels(h, g):
        return panel_v[h, g * GROUP : (g + 1) * GROUP].reshape(2 * GROUP * BLOCK, WIDE)

    ROWS = 256
    last = N_OFF // GROUP - 1
    sums = []
    for h in range(PARTS):
        for g in range(last):
            arrive(h, g)

            @pl.loop(0, NB * BLOCK // ROWS)
            def _(i):
                at = pl.ds(pl.multiple_of(i * ROWS, ROWS), ROWS)
                term = jnp.dot(dense_v[g, at, :], panels(h, g), preferred_element_type=jnp.float32)
                if g == 0:
                    total_v[at, :] = term
                else:
                    total_v[at, :] += term

        arrive(h, last)
        for d in range(1, NB + 1):
            b = lax.rem(q + d, NB)
            at = pl.ds(pl.multiple_of(b * BLOCK, BLOCK), BLOCK)
            full = total_v[at, :] + jnp.dot(dense_v[last, at, :], panels(h, last), preferred_element_type=jnp.float32)
            if d < NB:
                part_v[h, d] = full.astype(jnp.bfloat16)
                part = pltpu.make_async_remote_copy(
                    src_ref=part_v.at[h, d], dst_ref=land_v.at[h, d], send_sem=sum_send.at[h, d], recv_sem=sum_recv.at[h, d],
                    device_id=(r, b), device_id_type=MESH,
                )
                part.start()
                sums.append((h, d, part))
            else:
                rest_v[h] = full
    for h, d, part in sums:
        part.wait_recv()
        rest_v[h] += land_v[h, d].astype(jnp.float32)
    for h in range(PARTS):
        out_ref[:, h * WIDE : (h + 1) * WIDE] = rest_v[h].astype(jnp.bfloat16)
    for copy in spreads + asks + gives + [part for _, _, part in sums]:
        copy.wait_send()


def local(features, weight, tiles, tile_source, tile_target, live_tiles, wanted):
    vmem = pl.BlockSpec(memory_space=pltpu.VMEM)
    hbm = pl.BlockSpec(memory_space=pltpu.HBM)
    smem = pl.BlockSpec(memory_space=pltpu.SMEM)
    dma = pltpu.SemaphoreType.DMA
    bf16, f32, i32 = jnp.bfloat16, jnp.float32, jnp.int32
    return pl.pallas_call(
        kernel,
        out_shape=jax.ShapeDtypeStruct((BLOCK, F), bf16),
        in_specs=[smem, hbm, hbm, hbm, hbm, hbm, hbm],
        out_specs=vmem,
        scratch_shapes=[
            pltpu.VMEM((BLOCK, F), bf16),
            pltpu.VMEM((F, F), bf16),
            pltpu.VMEM((PARTS, BLOCK, WIDE), bf16),
            pltpu.VMEM((TILES + 1, BLOCK, BLOCK), bf16),
            pltpu.VMEM((N_OFF // GROUP, NB * BLOCK, 2 * GROUP * BLOCK), bf16),
            pltpu.VMEM((NB, BLOCK, WIDE), bf16),
            pltpu.VMEM((NB, BLOCK, WIDE), bf16),
            pltpu.VMEM((PARTS, 2 * N_OFF, BLOCK, WIDE), bf16),
            pltpu.VMEM((PARTS, N_OFF, 2, BLOCK, WIDE), bf16),
            pltpu.VMEM((NB * BLOCK, WIDE), f32),
            pltpu.VMEM((PARTS, BLOCK, WIDE), f32),
            pltpu.VMEM((PARTS, NB, BLOCK, WIDE), bf16),
            pltpu.VMEM((PARTS, NB, BLOCK, WIDE), bf16),
            pltpu.VMEM((1, TILES), i32),
            pltpu.VMEM((1, TILES), i32),
            pltpu.VMEM((1, SLABS), i32),
            pltpu.VMEM((1, 128), i32),
            pltpu.VMEM((2 * N_OFF, 1, 128), i32),
            pltpu.VMEM((1, NB * SLABS), i32),
            pltpu.SMEM((2 * N_OFF, 1, 128), i32),
            pltpu.SMEM((1, NB * SLABS), i32),
            dma((6,)), dma((3,)),
            dma((PARTS, NB)), dma((PARTS, NB)),
            dma((2 * N_OFF,)), dma((2 * N_OFF,)),
            dma((PARTS, 2 * N_OFF)), dma((PARTS, 2 * N_OFF)),
            dma((PARTS, NB)), dma((PARTS, NB)),
        ],
        compiler_params=pltpu.CompilerParams(
            collective_id=0, has_side_effects=True, vmem_limit_bytes=40 << 20
        ),
    )(
        live_tiles,
        *(
            pltpu.with_memory_space_constraint(operand, pltpu.HBM)
            for operand in (
                features, weight, tiles,
                tile_source.reshape(1, TILES), tile_target.reshape(1, TILES), wanted.reshape(1, SLABS),
            )
        ),
    )


def solution(mesh):
    placed = (
        P(("row", "rep"), None),
        P(),
        P("row", "rep", None, None, None),
        P("row", "rep", None),
        P("row", "rep", None),
        P("row", "rep"),
        P("row", "rep", None, None),
    )
    return jax.shard_map(
        local, mesh=mesh, in_specs=placed, out_specs=P(("row", "rep"), None), check_vma=False
    )
```

```python
import functools

import jax
import jax.numpy as jnp
from jax import lax
from jax.experimental import pallas as pl
from jax.experimental.pallas import tpu as pltpu
from jax.sharding import PartitionSpec as P

F = 256
BLOCK = 128
NB = 8
TILES = 128
SLABS = 32
GROUP = 16
MESH = pl.DeviceIdType.MESH

OFFSETS = [
    (1, 0, 1), (3, 0, 1), (0, 1, 1), (0, 3, 1),
    (0, 0, 1), (2, 0, 0), (0, 2, 0), (1, 1, 0),
    (3, 3, 0), (1, 3, 0), (3, 1, 0), (1, 0, 0),
    (3, 0, 0), (0, 1, 0), (0, 3, 0), (0, 0, 0),
]
HOME = OFFSETS.index((0, 0, 0))
N_OFF = len(OFFSETS)
PARTS = 2
WIDE = F // PARTS


def device(x, y, z, c):
    return (z * 4 + (y // 2) * 2 + c, lax.rem(y, 2) * 4 + x)


def owned_slab(x, y, z, c):
    odd = lax.rem(z, 2)
    zs = lax.rem(x + 2 * odd, 4) + 4 * lax.rem(y, 2)
    yh = lax.rem(y // 2 + odd + lax.rem(zs, 2) + 1, 2)
    return zs, yh


def owner_at(zs, yh, c, z):
    odd = lax.rem(z, 2)
    x = lax.rem(lax.rem(zs, 4) + 2 * odd, 4)
    pair = lax.rem(yh + odd + lax.rem(zs, 2) + 1, 2)
    return device(x, 2 * pair + zs // 4, z, c)


def kernel(
    live_ref, features_ref, weight_ref, tiles_ref, source_ref, target_ref, wanted_ref, out_ref,
    feat_v, weight_v, hidden_v, tiles_v, dense_v, slab_0_v, slab_1_v, picked_v, panel_v, total_v, rest_v, part_v, land_v,
    source_v, target_v, wanted_v, ask_v, req_v, slot_v, req_s, slot_s,
    load_sem, small_sem, spread_send, spread_recv, ask_send, ask_recv, give_send, give_recv, sum_send, sum_recv,
):
    slabs_v = (slab_0_v, slab_1_v)
    r, q = lax.axis_index("row"), lax.axis_index("rep")
    z, yh, c = r // 4, lax.rem(r // 2, 2), lax.rem(r, 2)
    yl, x = q // 4, lax.rem(q, 4)
    y = yh * 2 + yl

    loads = [
        pltpu.make_async_copy(features_ref, feat_v, load_sem.at[0]),
        pltpu.make_async_copy(weight_ref, weight_v, load_sem.at[1]),
        pltpu.make_async_copy(wanted_ref, wanted_v, load_sem.at[2]),
        pltpu.make_async_copy(source_ref, source_v, load_sem.at[3]),
        pltpu.make_async_copy(target_ref, target_v, load_sem.at[4]),
        pltpu.make_async_copy(tiles_ref.at[0, 0], tiles_v.at[pl.ds(0, TILES)], load_sem.at[5]),
    ]
    for load in loads:
        load.start()

    def owner_of(k, core):
        dx, dy, dz = OFFSETS[k]
        pz = lax.rem(z + dz * (1 - 2 * core) + 8, 8) if dz else z
        return lax.rem(x + dx, 4), lax.rem(y + dy, 4), pz, core

    def asker_of(k, core):
        dx, dy, dz = OFFSETS[k]
        pz = lax.rem(z - dz * (1 - 2 * c) + 8, 8) if dz else z
        return lax.rem(x + 4 - dx, 4), lax.rem(y + 4 - dy, 4), pz, core

    own_z, own_yh = owned_slab(x, y, z, c)
    own = own_z * 4 + own_yh * 2 + c

    barrier = pltpu.get_barrier_semaphore()
    n_signals = 0

    def tell(dev):
        pl.semaphore_signal(barrier, inc=1, device_id=dev, device_id_type=MESH)

    for b in range(NB):
        tell(device(b % 4, 2 * own_yh + b // 4, own_z, c))
    n_signals += NB
    for k in range(N_OFF):
        cores = (1 - c,) if k == HOME else (0, 1)
        for core in cores:
            tell(device(*asker_of(k, core)))
        n_signals += len(cores)

    loads[0].wait()
    loads[1].wait()
    hidden = jnp.dot(feat_v[...], weight_v[...], preferred_element_type=jnp.float32).astype(jnp.bfloat16)
    for h in range(PARTS):
        hidden_v[h] = hidden[:, h * WIDE : (h + 1) * WIDE]
    ask_v[...] = jnp.zeros_like(ask_v)
    loads[2].wait()
    ask_v[:, 0:SLABS] = wanted_v[...]

    pl.semaphore_wait(barrier, n_signals)

    spreads = []

    def spread_part(h):
        for dz in (0, 1, 7, 2, 6, 3, 5, 4):
            spread = pltpu.make_async_remote_copy(
                src_ref=hidden_v.at[h], dst_ref=slabs_v[h].at[q], send_sem=spread_send.at[h, dz], recv_sem=spread_recv.at[h, q],
                device_id=owner_at(z, yh, c, lax.rem(z + dz, 8)), device_id_type=MESH,
            )
            spread.start()
            spreads.append(spread)

    spread_part(0)
    asks = []
    for k in range(N_OFF):
        for core in (1 - c,) if k == HOME else (0, 1):
            ask = pltpu.make_async_remote_copy(
                src_ref=ask_v, dst_ref=req_v.at[2 * k + c], send_sem=ask_send.at[2 * k + core],
                recv_sem=ask_recv.at[2 * k + c], device_id=device(*owner_of(k, core)), device_id_type=MESH,
            )
            ask.start()
            asks.append(ask)
    for h in range(1, PARTS):
        spread_part(h)
    mine = pltpu.make_async_copy(ask_v, req_v.at[2 * HOME + c], small_sem.at[0])
    mine.start()

    loads[3].wait()
    loads[4].wait()
    t_row = lax.broadcasted_iota(jnp.int32, (1, TILES), 1)
    key = jnp.where(t_row < live_ref[0, 0], target_v[...] * SLABS + source_v[...], -1)
    here = lax.broadcasted_iota(jnp.int32, (TILES, TILES), 0) == lax.broadcasted_iota(jnp.int32, (TILES, TILES), 1)
    column = jnp.sum(jnp.where(here, jnp.broadcast_to(key, (TILES, TILES)), 0), axis=1, keepdims=True)
    pair = lax.broadcasted_iota(jnp.int32, (TILES, NB * SLABS), 1)
    slot = lax.broadcasted_iota(jnp.int32, (TILES, NB * SLABS), 0)
    found = jnp.where(jnp.broadcast_to(column, (TILES, NB * SLABS)) == pair, slot - TILES, 0)
    slot_v[...] = jnp.sum(found, axis=0, keepdims=True) + TILES
    to_scalar = pltpu.make_async_copy(slot_v, slot_s, small_sem.at[1])
    to_scalar.start()
    tiles_v[TILES] = jnp.zeros((BLOCK, BLOCK), jnp.bfloat16)
    loads[5].wait()
    to_scalar.wait()

    def place(k):
        for core in (0, 1):
            px, py, pz, _ = owner_of(k, core)
            sz, syh = owned_slab(px, py, pz, core)
            s = sz * 4 + syh * 2 + core
            at = (k % GROUP) * 2 * BLOCK + core * BLOCK

            @pl.loop(0, NB)
            def _(b):
                rows = pl.ds(pl.multiple_of(b * BLOCK, BLOCK), BLOCK)
                dense_v[k // GROUP, rows, at : at + BLOCK] = tiles_v[slot_s[0, b * SLABS + s]]

    for k in range(N_OFF):
        place(k)

    mine.wait()
    for k in range(N_OFF):
        for core in (1 - c,) if k == HOME else (0, 1):
            pltpu.make_async_remote_copy(
                src_ref=ask_v, dst_ref=req_v.at[2 * k + core], send_sem=ask_send.at[2 * k + core],
                recv_sem=ask_recv.at[2 * k + core], device_id=device(*asker_of(k, core)), device_id_type=MESH,
            ).wait_recv()
    to_scalar = pltpu.make_async_copy(req_v, req_s, small_sem.at[2])
    to_scalar.start()
    to_scalar.wait()

    gives = []
    for h in range(PARTS):
        for b in range(NB):
            pltpu.make_async_remote_copy(
                src_ref=hidden_v.at[h], dst_ref=slabs_v[h].at[b], send_sem=spread_send.at[h, b], recv_sem=spread_recv.at[h, b],
                device_id=device(b % 4, 2 * own_yh + b // 4, own_z, c), device_id_type=MESH,
            ).wait_recv()
        for k in range(N_OFF):
            for core in (1 - c,) if k == HOME else (0, 1):
                index = 2 * k + core
                picked_v[h, index] = slabs_v[h][req_s[index, 0, own]]
                give = pltpu.make_async_remote_copy(
                    src_ref=picked_v.at[h, index], dst_ref=panel_v.at[h, k, c], send_sem=give_send.at[h, index],
                    recv_sem=give_recv.at[h, 2 * k + c], device_id=device(*asker_of(k, core)), device_id_type=MESH,
                )
                give.start()
                gives.append(give)
        panel_v[h, HOME, c] = slabs_v[h][req_s[2 * HOME + c, 0, own]]

    def arrive(h, g):
        for k in range(g * GROUP, (g + 1) * GROUP):
            for core in (1 - c,) if k == HOME else (0, 1):
                pltpu.make_async_remote_copy(
                    src_ref=picked_v.at[h, 0], dst_ref=panel_v.at[h, k, core], send_sem=give_send.at[h, 2 * k + core],
                    recv_sem=give_recv.at[h, 2 * k + core], device_id=device(*owner_of(k, core)), device_id_type=MESH,
                ).wait_recv()

    def panels(h, g):
        return panel_v[h, g * GROUP : (g + 1) * GROUP].reshape(2 * GROUP * BLOCK, WIDE)

    ROWS = 256
    last = N_OFF // GROUP - 1
    sums = []
    for h in range(PARTS):
        for g in range(last):
            arrive(h, g)

            @pl.loop(0, NB * BLOCK // ROWS)
            def _(i):
                at = pl.ds(pl.multiple_of(i * ROWS, ROWS), ROWS)
                term = jnp.dot(dense_v[g, at, :], panels(h, g), preferred_element_type=jnp.float32)
                if g == 0:
                    total_v[at, :] = term
                else:
                    total_v[at, :] += term

        arrive(h, last)
        for d in range(1, NB + 1):
            b = lax.rem(q + d, NB)
            at = pl.ds(pl.multiple_of(b * BLOCK, BLOCK), BLOCK)
            full = total_v[at, :] + jnp.dot(dense_v[last, at, :], panels(h, last), preferred_element_type=jnp.float32)
            if d < NB:
                part_v[h, d] = full.astype(jnp.bfloat16)
                part = pltpu.make_async_remote_copy(
                    src_ref=part_v.at[h, d], dst_ref=land_v.at[h, d], send_sem=sum_send.at[h, d], recv_sem=sum_recv.at[h, d],
                    device_id=(r, b), device_id_type=MESH,
                )
                part.start()
                sums.append((h, d, part))
            else:
                rest_v[h] = full
    for copy in spreads + asks + gives:
        copy.wait_send()
    for h, d, part in sums:
        part.wait_recv()
        rest_v[h] += land_v[h, d].astype(jnp.float32)
    for h in range(PARTS):
        out_ref[:, h * WIDE : (h + 1) * WIDE] = rest_v[h].astype(jnp.bfloat16)
    for _, _, part in sums:
        part.wait_send()


def local(features, weight, tiles, tile_source, tile_target, live_tiles, wanted):
    vmem = pl.BlockSpec(memory_space=pltpu.VMEM)
    hbm = pl.BlockSpec(memory_space=pltpu.HBM)
    smem = pl.BlockSpec(memory_space=pltpu.SMEM)
    dma = pltpu.SemaphoreType.DMA
    bf16, f32, i32 = jnp.bfloat16, jnp.float32, jnp.int32
    return pl.pallas_call(
        kernel,
        out_shape=jax.ShapeDtypeStruct((BLOCK, F), bf16),
        in_specs=[smem, hbm, hbm, hbm, hbm, hbm, hbm],
        out_specs=vmem,
        scratch_shapes=[
            pltpu.VMEM((BLOCK, F), bf16),
            pltpu.VMEM((F, F), bf16),
            pltpu.VMEM((PARTS, BLOCK, WIDE), bf16),
            pltpu.VMEM((TILES + 1, BLOCK, BLOCK), bf16),
            pltpu.VMEM((N_OFF // GROUP, NB * BLOCK, 2 * GROUP * BLOCK), bf16),
            pltpu.VMEM((NB, BLOCK, WIDE), bf16),
            pltpu.VMEM((NB, BLOCK, WIDE), bf16),
            pltpu.VMEM((PARTS, 2 * N_OFF, BLOCK, WIDE), bf16),
            pltpu.VMEM((PARTS, N_OFF, 2, BLOCK, WIDE), bf16),
            pltpu.VMEM((NB * BLOCK, WIDE), f32),
            pltpu.VMEM((PARTS, BLOCK, WIDE), f32),
            pltpu.VMEM((PARTS, NB, BLOCK, WIDE), bf16),
            pltpu.VMEM((PARTS, NB, BLOCK, WIDE), bf16),
            pltpu.VMEM((1, TILES), i32),
            pltpu.VMEM((1, TILES), i32),
            pltpu.VMEM((1, SLABS), i32),
            pltpu.VMEM((1, 128), i32),
            pltpu.VMEM((2 * N_OFF, 1, 128), i32),
            pltpu.VMEM((1, NB * SLABS), i32),
            pltpu.SMEM((2 * N_OFF, 1, 128), i32),
            pltpu.SMEM((1, NB * SLABS), i32),
            dma((6,)), dma((3,)),
            dma((PARTS, NB)), dma((PARTS, NB)),
            dma((2 * N_OFF,)), dma((2 * N_OFF,)),
            dma((PARTS, 2 * N_OFF)), dma((PARTS, 2 * N_OFF)),
            dma((PARTS, NB)), dma((PARTS, NB)),
        ],
        compiler_params=pltpu.CompilerParams(
            collective_id=0, has_side_effects=True, vmem_limit_bytes=40 << 20
        ),
    )(
        live_tiles,
        *(
            pltpu.with_memory_space_constraint(operand, pltpu.HBM)
            for operand in (
                features, weight, tiles,
                tile_source.reshape(1, TILES), tile_target.reshape(1, TILES), wanted.reshape(1, SLABS),
            )
        ),
    )


def solution(mesh):
    placed = (
        P(("row", "rep"), None),
        P(),
        P("row", "rep", None, None, None),
        P("row", "rep", None),
        P("row", "rep", None),
        P("row", "rep"),
        P("row", "rep", None, None),
    )
    return jax.shard_map(
        local, mesh=mesh, in_specs=placed, out_specs=P(("row", "rep"), None), check_vma=False
    )
```

```python
import functools

import jax
import jax.numpy as jnp
from jax import lax
from jax.experimental import pallas as pl
from jax.experimental.pallas import tpu as pltpu
from jax.sharding import PartitionSpec as P

F = 256
BLOCK = 128
NB = 8
TILES = 128
SLABS = 32
GROUP = 16
MESH = pl.DeviceIdType.MESH

OFFSETS = [
    (1, 0, 1), (3, 0, 1), (0, 1, 1), (0, 3, 1),
    (0, 0, 1), (2, 0, 0), (0, 2, 0), (1, 1, 0),
    (3, 3, 0), (1, 3, 0), (3, 1, 0), (1, 0, 0),
    (3, 0, 0), (0, 1, 0), (0, 3, 0), (0, 0, 0),
]
HOME = OFFSETS.index((0, 0, 0))
N_OFF = len(OFFSETS)
PARTS = 2
WIDE = F // PARTS


def device(x, y, z, c):
    return (z * 4 + (y // 2) * 2 + c, lax.rem(y, 2) * 4 + x)


def owned_slab(x, y, z, c):
    odd = lax.rem(z, 2)
    zs = lax.rem(x + 2 * odd, 4) + 4 * lax.rem(y, 2)
    yh = lax.rem(y // 2 + odd + lax.rem(zs, 2) + 1, 2)
    return zs, yh


def owner_at(zs, yh, c, z):
    odd = lax.rem(z, 2)
    x = lax.rem(lax.rem(zs, 4) + 2 * odd, 4)
    pair = lax.rem(yh + odd + lax.rem(zs, 2) + 1, 2)
    return device(x, 2 * pair + zs // 4, z, c)


def kernel(
    live_ref, features_ref, weight_ref, tiles_ref, source_ref, target_ref, wanted_ref, out_ref,
    feat_v, weight_v, hidden_v, tiles_v, dense_v, slab_0_v, slab_1_v, picked_v, panel_v, rest_v, part_v, land_v,
    source_v, target_v, wanted_v, ask_v, req_v, slot_v, req_s, slot_s,
    load_sem, small_sem, spread_send, spread_recv, ask_send, ask_recv, give_send, give_recv, sum_send, sum_recv,
):
    slabs_v = (slab_0_v, slab_1_v)
    r, q = lax.axis_index("row"), lax.axis_index("rep")
    z, yh, c = r // 4, lax.rem(r // 2, 2), lax.rem(r, 2)
    yl, x = q // 4, lax.rem(q, 4)
    y = yh * 2 + yl

    loads = [
        pltpu.make_async_copy(features_ref, feat_v, load_sem.at[0]),
        pltpu.make_async_copy(weight_ref, weight_v, load_sem.at[1]),
        pltpu.make_async_copy(wanted_ref, wanted_v, load_sem.at[2]),
        pltpu.make_async_copy(source_ref, source_v, load_sem.at[3]),
        pltpu.make_async_copy(target_ref, target_v, load_sem.at[4]),
        pltpu.make_async_copy(tiles_ref.at[0, 0], tiles_v.at[pl.ds(0, TILES)], load_sem.at[5]),
    ]
    for load in loads:
        load.start()

    def owner_of(k, core):
        dx, dy, dz = OFFSETS[k]
        pz = lax.rem(z + dz * (1 - 2 * core) + 8, 8) if dz else z
        return lax.rem(x + dx, 4), lax.rem(y + dy, 4), pz, core

    def asker_of(k, core):
        dx, dy, dz = OFFSETS[k]
        pz = lax.rem(z - dz * (1 - 2 * c) + 8, 8) if dz else z
        return lax.rem(x + 4 - dx, 4), lax.rem(y + 4 - dy, 4), pz, core

    own_z, own_yh = owned_slab(x, y, z, c)
    own = own_z * 4 + own_yh * 2 + c

    barrier = pltpu.get_barrier_semaphore()
    n_signals = 0

    def tell(dev):
        pl.semaphore_signal(barrier, inc=1, device_id=dev, device_id_type=MESH)

    for b in range(NB):
        tell(device(b % 4, 2 * own_yh + b // 4, own_z, c))
    n_signals += NB
    for k in range(N_OFF):
        cores = (1 - c,) if k == HOME else (0, 1)
        for core in cores:
            tell(device(*asker_of(k, core)))
        n_signals += len(cores)

    loads[0].wait()
    loads[1].wait()
    hidden = jnp.dot(feat_v[...], weight_v[...], preferred_element_type=jnp.float32).astype(jnp.bfloat16)
    for h in range(PARTS):
        hidden_v[h] = hidden[:, h * WIDE : (h + 1) * WIDE]
    ask_v[...] = jnp.zeros_like(ask_v)
    loads[2].wait()
    ask_v[:, 0:SLABS] = wanted_v[...]

    pl.semaphore_wait(barrier, n_signals)

    spreads = []

    def spread_part(h):
        for dz in (0, 1, 7, 2, 6, 3, 5, 4) if h == 0 else (4, 3, 5, 2, 6, 1, 7, 0):
            spread = pltpu.make_async_remote_copy(
                src_ref=hidden_v.at[h], dst_ref=slabs_v[h].at[q], send_sem=spread_send.at[h, dz], recv_sem=spread_recv.at[h, q],
                device_id=owner_at(z, yh, c, lax.rem(z + dz, 8)), device_id_type=MESH,
            )
            spread.start()
            spreads.append(spread)

    spread_part(0)
    asks = []
    for k in range(N_OFF):
        for core in (1 - c,) if k == HOME else (0, 1):
            ask = pltpu.make_async_remote_copy(
                src_ref=ask_v, dst_ref=req_v.at[2 * k + c], send_sem=ask_send.at[2 * k + core],
                recv_sem=ask_recv.at[2 * k + c], device_id=device(*owner_of(k, core)), device_id_type=MESH,
            )
            ask.start()
            asks.append(ask)
    for h in range(1, PARTS):
        spread_part(h)
    mine = pltpu.make_async_copy(ask_v, req_v.at[2 * HOME + c], small_sem.at[0])
    mine.start()

    loads[3].wait()
    loads[4].wait()
    t_row = lax.broadcasted_iota(jnp.int32, (1, TILES), 1)
    key = jnp.where(t_row < live_ref[0, 0], target_v[...] * SLABS + source_v[...], -1)
    here = lax.broadcasted_iota(jnp.int32, (TILES, TILES), 0) == lax.broadcasted_iota(jnp.int32, (TILES, TILES), 1)
    column = jnp.sum(jnp.where(here, jnp.broadcast_to(key, (TILES, TILES)), 0), axis=1, keepdims=True)
    pair = lax.broadcasted_iota(jnp.int32, (TILES, NB * SLABS), 1)
    slot = lax.broadcasted_iota(jnp.int32, (TILES, NB * SLABS), 0)
    found = jnp.where(jnp.broadcast_to(column, (TILES, NB * SLABS)) == pair, slot - TILES, 0)
    slot_v[...] = jnp.sum(found, axis=0, keepdims=True) + TILES
    to_scalar = pltpu.make_async_copy(slot_v, slot_s, small_sem.at[1])
    to_scalar.start()
    tiles_v[TILES] = jnp.zeros((BLOCK, BLOCK), jnp.bfloat16)
    loads[5].wait()
    to_scalar.wait()

    def place(k):
        for core in (0, 1):
            px, py, pz, _ = owner_of(k, core)
            sz, syh = owned_slab(px, py, pz, core)
            s = sz * 4 + syh * 2 + core
            at = (k % GROUP) * 2 * BLOCK + core * BLOCK

            @pl.loop(0, NB)
            def _(b):
                rows = pl.ds(pl.multiple_of(b * BLOCK, BLOCK), BLOCK)
                dense_v[k // GROUP, rows, at : at + BLOCK] = tiles_v[slot_s[0, b * SLABS + s]]

    for k in range(N_OFF):
        place(k)

    mine.wait()
    for k in range(N_OFF):
        for core in (1 - c,) if k == HOME else (0, 1):
            pltpu.make_async_remote_copy(
                src_ref=ask_v, dst_ref=req_v.at[2 * k + core], send_sem=ask_send.at[2 * k + core],
                recv_sem=ask_recv.at[2 * k + core], device_id=device(*asker_of(k, core)), device_id_type=MESH,
            ).wait_recv()
    to_scalar = pltpu.make_async_copy(req_v, req_s, small_sem.at[2])
    to_scalar.start()
    to_scalar.wait()

    gives = []
    for h in range(PARTS):
        for b in range(NB):
            pltpu.make_async_remote_copy(
                src_ref=hidden_v.at[h], dst_ref=slabs_v[h].at[b], send_sem=spread_send.at[h, b], recv_sem=spread_recv.at[h, b],
                device_id=device(b % 4, 2 * own_yh + b // 4, own_z, c), device_id_type=MESH,
            ).wait_recv()
        for k in range(N_OFF):
            for core in (1 - c,) if k == HOME else (0, 1):
                index = 2 * k + core
                picked_v[h, index] = slabs_v[h][req_s[index, 0, own]]
                give = pltpu.make_async_remote_copy(
                    src_ref=picked_v.at[h, index], dst_ref=panel_v.at[h, k, c], send_sem=give_send.at[h, index],
                    recv_sem=give_recv.at[h, 2 * k + c], device_id=device(*asker_of(k, core)), device_id_type=MESH,
                )
                give.start()
                gives.append(give)
        panel_v[h, HOME, c] = slabs_v[h][req_s[2 * HOME + c, 0, own]]

    def arrive(h, g):
        for k in range(g * GROUP, (g + 1) * GROUP):
            for core in (1 - c,) if k == HOME else (0, 1):
                pltpu.make_async_remote_copy(
                    src_ref=picked_v.at[h, 0], dst_ref=panel_v.at[h, k, core], send_sem=give_send.at[h, 2 * k + core],
                    recv_sem=give_recv.at[h, 2 * k + core], device_id=device(*owner_of(k, core)), device_id_type=MESH,
                ).wait_recv()

    def panels(h, g):
        return panel_v[h, g * GROUP : (g + 1) * GROUP].reshape(2 * GROUP * BLOCK, WIDE)

    last = N_OFF // GROUP - 1
    sums = []
    for h in range(PARTS):
        arrive(h, last)

        def full(b):
            at = pl.ds(pl.multiple_of(b * BLOCK, BLOCK), BLOCK)
            return jnp.dot(dense_v[0, at, :], panels(h, 0), preferred_element_type=jnp.float32)

        def part_to(d, h=h):
            return pltpu.make_async_remote_copy(
                src_ref=part_v.at[h, d], dst_ref=land_v.at[h, d], send_sem=sum_send.at[h, d], recv_sem=sum_recv.at[h, d],
                device_id=(r, lax.rem(q + d, NB)), device_id_type=MESH,
            )

        @pl.loop(1, NB)
        def _(d):
            part_v[h, d] = full(lax.rem(q + d, NB)).astype(jnp.bfloat16)
            part_to(d).start()

        rest_v[h] = full(q)
        sums += [(h, d, part_to(d)) for d in range(1, NB)]
    for copy in spreads + asks + gives:
        copy.wait_send()
    for h, d, part in sums:
        part.wait_recv()
        rest_v[h] += land_v[h, d].astype(jnp.float32)
    for h in range(PARTS):
        out_ref[:, h * WIDE : (h + 1) * WIDE] = rest_v[h].astype(jnp.bfloat16)
    for _, _, part in sums:
        part.wait_send()


def local(features, weight, tiles, tile_source, tile_target, live_tiles, wanted):
    vmem = pl.BlockSpec(memory_space=pltpu.VMEM)
    hbm = pl.BlockSpec(memory_space=pltpu.HBM)
    smem = pl.BlockSpec(memory_space=pltpu.SMEM)
    dma = pltpu.SemaphoreType.DMA
    bf16, f32, i32 = jnp.bfloat16, jnp.float32, jnp.int32
    return pl.pallas_call(
        kernel,
        out_shape=jax.ShapeDtypeStruct((BLOCK, F), bf16),
        in_specs=[smem, hbm, hbm, hbm, hbm, hbm, hbm],
        out_specs=vmem,
        scratch_shapes=[
            pltpu.VMEM((BLOCK, F), bf16),
            pltpu.VMEM((F, F), bf16),
            pltpu.VMEM((PARTS, BLOCK, WIDE), bf16),
            pltpu.VMEM((TILES + 1, BLOCK, BLOCK), bf16),
            pltpu.VMEM((N_OFF // GROUP, NB * BLOCK, 2 * GROUP * BLOCK), bf16),
            pltpu.VMEM((NB, BLOCK, WIDE), bf16),
            pltpu.VMEM((NB, BLOCK, WIDE), bf16),
            pltpu.VMEM((PARTS, 2 * N_OFF, BLOCK, WIDE), bf16),
            pltpu.VMEM((PARTS, N_OFF, 2, BLOCK, WIDE), bf16),
            pltpu.VMEM((PARTS, BLOCK, WIDE), f32),
            pltpu.VMEM((PARTS, NB, BLOCK, WIDE), bf16),
            pltpu.VMEM((PARTS, NB, BLOCK, WIDE), bf16),
            pltpu.VMEM((1, TILES), i32),
            pltpu.VMEM((1, TILES), i32),
            pltpu.VMEM((1, SLABS), i32),
            pltpu.VMEM((1, 128), i32),
            pltpu.VMEM((2 * N_OFF, 1, 128), i32),
            pltpu.VMEM((1, NB * SLABS), i32),
            pltpu.SMEM((2 * N_OFF, 1, 128), i32),
            pltpu.SMEM((1, NB * SLABS), i32),
            dma((6,)), dma((3,)),
            dma((PARTS, NB)), dma((PARTS, NB)),
            dma((2 * N_OFF,)), dma((2 * N_OFF,)),
            dma((PARTS, 2 * N_OFF)), dma((PARTS, 2 * N_OFF)),
            dma((PARTS, NB)), dma((PARTS, NB)),
        ],
        compiler_params=pltpu.CompilerParams(
            collective_id=0, has_side_effects=True, vmem_limit_bytes=40 << 20
        ),
    )(
        live_tiles,
        *(
            pltpu.with_memory_space_constraint(operand, pltpu.HBM)
            for operand in (
                features, weight, tiles,
                tile_source.reshape(1, TILES), tile_target.reshape(1, TILES), wanted.reshape(1, SLABS),
            )
        ),
    )


def solution(mesh):
    placed = (
        P(("row", "rep"), None),
        P(),
        P("row", "rep", None, None, None),
        P("row", "rep", None),
        P("row", "rep", None),
        P("row", "rep"),
        P("row", "rep", None, None),
    )
    return jax.shard_map(
        local, mesh=mesh, in_specs=placed, out_specs=P(("row", "rep"), None), check_vma=False
    )
```

```python
import functools

import jax
import jax.numpy as jnp
from jax import lax
from jax.experimental import pallas as pl
from jax.experimental.pallas import tpu as pltpu
from jax.sharding import PartitionSpec as P

F = 256
BLOCK = 128
NB = 8
TILES = 128
SLABS = 32
GROUP = 16
MESH = pl.DeviceIdType.MESH

OFFSETS = [
    (1, 0, 1), (3, 0, 1), (0, 1, 1), (0, 3, 1),
    (0, 0, 1), (2, 0, 0), (0, 2, 0), (1, 1, 0),
    (3, 3, 0), (1, 3, 0), (3, 1, 0), (1, 0, 0),
    (3, 0, 0), (0, 1, 0), (0, 3, 0), (0, 0, 0),
]
HOME = OFFSETS.index((0, 0, 0))
N_OFF = len(OFFSETS)
PARTS = 2
WIDE = F // PARTS


def device(x, y, z, c):
    return (z * 4 + (y // 2) * 2 + c, lax.rem(y, 2) * 4 + x)


def owned_slab(x, y, z, c):
    odd = lax.rem(z, 2)
    zs = lax.rem(x + 2 * odd, 4) + 4 * lax.rem(y, 2)
    yh = lax.rem(y // 2 + odd + lax.rem(zs, 2) + 1, 2)
    return zs, yh


def owner_at(zs, yh, c, z):
    odd = lax.rem(z, 2)
    x = lax.rem(lax.rem(zs, 4) + 2 * odd, 4)
    pair = lax.rem(yh + odd + lax.rem(zs, 2) + 1, 2)
    return device(x, 2 * pair + zs // 4, z, c)


def kernel(
    live_ref, features_ref, weight_ref, tiles_ref, source_ref, target_ref, wanted_ref, out_ref,
    feat_v, weight_v, hidden_v, tiles_v, dense_v, slab_0_v, slab_1_v, picked_v, panel_v, rest_v, part_v, land_v,
    source_v, target_v, wanted_v, ask_v, req_v, slot_v, req_s, slot_s,
    load_sem, small_sem, spread_send, spread_recv, ask_send, ask_recv, give_send, give_recv, sum_send, sum_recv,
):
    slabs_v = (slab_0_v, slab_1_v)
    r, q = lax.axis_index("row"), lax.axis_index("rep")
    z, yh, c = r // 4, lax.rem(r // 2, 2), lax.rem(r, 2)
    yl, x = q // 4, lax.rem(q, 4)
    y = yh * 2 + yl

    loads = [
        pltpu.make_async_copy(features_ref, feat_v, load_sem.at[0]),
        pltpu.make_async_copy(weight_ref, weight_v, load_sem.at[1]),
        pltpu.make_async_copy(wanted_ref, wanted_v, load_sem.at[2]),
        pltpu.make_async_copy(source_ref, source_v, load_sem.at[3]),
        pltpu.make_async_copy(target_ref, target_v, load_sem.at[4]),
        pltpu.make_async_copy(tiles_ref.at[0, 0], tiles_v.at[pl.ds(0, TILES)], load_sem.at[5]),
    ]
    for load in loads:
        load.start()

    def owner_of(k, core):
        dx, dy, dz = OFFSETS[k]
        pz = lax.rem(z + dz * (1 - 2 * core) + 8, 8) if dz else z
        return lax.rem(x + dx, 4), lax.rem(y + dy, 4), pz, core

    def asker_of(k, core):
        dx, dy, dz = OFFSETS[k]
        pz = lax.rem(z - dz * (1 - 2 * c) + 8, 8) if dz else z
        return lax.rem(x + 4 - dx, 4), lax.rem(y + 4 - dy, 4), pz, core

    own_z, own_yh = owned_slab(x, y, z, c)
    own = own_z * 4 + own_yh * 2 + c

    barrier = pltpu.get_barrier_semaphore()
    n_signals = 0

    def tell(dev):
        pl.semaphore_signal(barrier, inc=1, device_id=dev, device_id_type=MESH)

    for b in range(NB):
        tell(device(b % 4, 2 * own_yh + b // 4, own_z, c))
    n_signals += NB
    for k in range(N_OFF):
        cores = (1 - c,) if k == HOME else (0, 1)
        for core in cores:
            tell(device(*asker_of(k, core)))
        n_signals += len(cores)

    loads[0].wait()
    loads[1].wait()
    hidden = jnp.dot(feat_v[...], weight_v[...], preferred_element_type=jnp.float32).astype(jnp.bfloat16)
    for h in range(PARTS):
        hidden_v[h] = hidden[:, h * WIDE : (h + 1) * WIDE]
    ask_v[...] = jnp.zeros_like(ask_v)
    loads[2].wait()
    ask_v[:, 0:SLABS] = wanted_v[...]

    pl.semaphore_wait(barrier, n_signals)

    spreads = []

    def spread_part(h, order=(4, 3, 5, 2, 6, 1, 7, 0)):
        for dz in order:
            spread = pltpu.make_async_remote_copy(
                src_ref=hidden_v.at[h], dst_ref=slabs_v[h].at[q], send_sem=spread_send.at[h, dz], recv_sem=spread_recv.at[h, q],
                device_id=owner_at(z, yh, c, lax.rem(z + dz, 8)), device_id_type=MESH,
            )
            spread.start()
            spreads.append(spread)

    spread_part(0, (0, 1, 7, 4))
    asks = []
    for k in range(N_OFF):
        for core in (1 - c,) if k == HOME else (0, 1):
            ask = pltpu.make_async_remote_copy(
                src_ref=ask_v, dst_ref=req_v.at[2 * k + c], send_sem=ask_send.at[2 * k + core],
                recv_sem=ask_recv.at[2 * k + c], device_id=device(*owner_of(k, core)), device_id_type=MESH,
            )
            ask.start()
            asks.append(ask)
    spread_part(0, (2, 6, 3, 5))
    for h in range(1, PARTS):
        spread_part(h)
    mine = pltpu.make_async_copy(ask_v, req_v.at[2 * HOME + c], small_sem.at[0])
    mine.start()

    loads[3].wait()
    loads[4].wait()
    t_row = lax.broadcasted_iota(jnp.int32, (1, TILES), 1)
    key = jnp.where(t_row < live_ref[0, 0], target_v[...] * SLABS + source_v[...], -1)
    here = lax.broadcasted_iota(jnp.int32, (TILES, TILES), 0) == lax.broadcasted_iota(jnp.int32, (TILES, TILES), 1)
    column = jnp.sum(jnp.where(here, jnp.broadcast_to(key, (TILES, TILES)), 0), axis=1, keepdims=True)
    pair = lax.broadcasted_iota(jnp.int32, (TILES, NB * SLABS), 1)
    slot = lax.broadcasted_iota(jnp.int32, (TILES, NB * SLABS), 0)
    found = jnp.where(jnp.broadcast_to(column, (TILES, NB * SLABS)) == pair, slot - TILES, 0)
    slot_v[...] = jnp.sum(found, axis=0, keepdims=True) + TILES
    to_scalar = pltpu.make_async_copy(slot_v, slot_s, small_sem.at[1])
    to_scalar.start()
    tiles_v[TILES] = jnp.zeros((BLOCK, BLOCK), jnp.bfloat16)
    loads[5].wait()
    to_scalar.wait()

    def place(k):
        for core in (0, 1):
            px, py, pz, _ = owner_of(k, core)
            sz, syh = owned_slab(px, py, pz, core)
            s = sz * 4 + syh * 2 + core
            at = (k % GROUP) * 2 * BLOCK + core * BLOCK

            @pl.loop(0, NB)
            def _(b):
                rows = pl.ds(pl.multiple_of(b * BLOCK, BLOCK), BLOCK)
                dense_v[k // GROUP, rows, at : at + BLOCK] = tiles_v[slot_s[0, b * SLABS + s]]

    for k in range(N_OFF):
        place(k)

    mine.wait()
    for k in range(N_OFF):
        for core in (1 - c,) if k == HOME else (0, 1):
            pltpu.make_async_remote_copy(
                src_ref=ask_v, dst_ref=req_v.at[2 * k + core], send_sem=ask_send.at[2 * k + core],
                recv_sem=ask_recv.at[2 * k + core], device_id=device(*asker_of(k, core)), device_id_type=MESH,
            ).wait_recv()
    to_scalar = pltpu.make_async_copy(req_v, req_s, small_sem.at[2])
    to_scalar.start()
    to_scalar.wait()

    gives = []
    for h in range(PARTS):
        for b in range(NB):
            pltpu.make_async_remote_copy(
                src_ref=hidden_v.at[h], dst_ref=slabs_v[h].at[b], send_sem=spread_send.at[h, b], recv_sem=spread_recv.at[h, b],
                device_id=device(b % 4, 2 * own_yh + b // 4, own_z, c), device_id_type=MESH,
            ).wait_recv()
        for k in range(N_OFF):
            for core in (1 - c,) if k == HOME else (0, 1):
                index = 2 * k + core
                picked_v[h, index] = slabs_v[h][req_s[index, 0, own]]
                give = pltpu.make_async_remote_copy(
                    src_ref=picked_v.at[h, index], dst_ref=panel_v.at[h, k, c], send_sem=give_send.at[h, index],
                    recv_sem=give_recv.at[h, 2 * k + c], device_id=device(*asker_of(k, core)), device_id_type=MESH,
                )
                give.start()
                gives.append(give)
        panel_v[h, HOME, c] = slabs_v[h][req_s[2 * HOME + c, 0, own]]

    def arrive(h, g):
        for k in range(g * GROUP, (g + 1) * GROUP):
            for core in (1 - c,) if k == HOME else (0, 1):
                pltpu.make_async_remote_copy(
                    src_ref=picked_v.at[h, 0], dst_ref=panel_v.at[h, k, core], send_sem=give_send.at[h, 2 * k + core],
                    recv_sem=give_recv.at[h, 2 * k + core], device_id=device(*owner_of(k, core)), device_id_type=MESH,
                ).wait_recv()

    def panels(h, g):
        return panel_v[h, g * GROUP : (g + 1) * GROUP].reshape(2 * GROUP * BLOCK, WIDE)

    last = N_OFF // GROUP - 1
    sums = []
    for h in range(PARTS):
        arrive(h, last)

        def full(b):
            at = pl.ds(pl.multiple_of(b * BLOCK, BLOCK), BLOCK)
            return jnp.dot(dense_v[0, at, :], panels(h, 0), preferred_element_type=jnp.float32)

        def part_to(d, h=h):
            return pltpu.make_async_remote_copy(
                src_ref=part_v.at[h, d], dst_ref=land_v.at[h, d], send_sem=sum_send.at[h, d], recv_sem=sum_recv.at[h, d],
                device_id=(r, lax.rem(q + d, NB)), device_id_type=MESH,
            )

        @pl.loop(1, NB)
        def _(d):
            part_v[h, d] = full(lax.rem(q + d, NB)).astype(jnp.bfloat16)
            part_to(d).start()

        rest_v[h] = full(q)
        sums += [(h, d, part_to(d)) for d in range(1, NB)]
    for copy in spreads + asks + gives:
        copy.wait_send()
    for h, d, part in sums:
        part.wait_recv()
        rest_v[h] += land_v[h, d].astype(jnp.float32)
    for h in range(PARTS):
        out_ref[:, h * WIDE : (h + 1) * WIDE] = rest_v[h].astype(jnp.bfloat16)
    for _, _, part in sums:
        part.wait_send()


def local(features, weight, tiles, tile_source, tile_target, live_tiles, wanted):
    vmem = pl.BlockSpec(memory_space=pltpu.VMEM)
    hbm = pl.BlockSpec(memory_space=pltpu.HBM)
    smem = pl.BlockSpec(memory_space=pltpu.SMEM)
    dma = pltpu.SemaphoreType.DMA
    bf16, f32, i32 = jnp.bfloat16, jnp.float32, jnp.int32
    return pl.pallas_call(
        kernel,
        out_shape=jax.ShapeDtypeStruct((BLOCK, F), bf16),
        in_specs=[smem, hbm, hbm, hbm, hbm, hbm, hbm],
        out_specs=vmem,
        scratch_shapes=[
            pltpu.VMEM((BLOCK, F), bf16),
            pltpu.VMEM((F, F), bf16),
            pltpu.VMEM((PARTS, BLOCK, WIDE), bf16),
            pltpu.VMEM((TILES + 1, BLOCK, BLOCK), bf16),
            pltpu.VMEM((N_OFF // GROUP, NB * BLOCK, 2 * GROUP * BLOCK), bf16),
            pltpu.VMEM((NB, BLOCK, WIDE), bf16),
            pltpu.VMEM((NB, BLOCK, WIDE), bf16),
            pltpu.VMEM((PARTS, 2 * N_OFF, BLOCK, WIDE), bf16),
            pltpu.VMEM((PARTS, N_OFF, 2, BLOCK, WIDE), bf16),
            pltpu.VMEM((PARTS, BLOCK, WIDE), f32),
            pltpu.VMEM((PARTS, NB, BLOCK, WIDE), bf16),
            pltpu.VMEM((PARTS, NB, BLOCK, WIDE), bf16),
            pltpu.VMEM((1, TILES), i32),
            pltpu.VMEM((1, TILES), i32),
            pltpu.VMEM((1, SLABS), i32),
            pltpu.VMEM((1, 128), i32),
            pltpu.VMEM((2 * N_OFF, 1, 128), i32),
            pltpu.VMEM((1, NB * SLABS), i32),
            pltpu.SMEM((2 * N_OFF, 1, 128), i32),
            pltpu.SMEM((1, NB * SLABS), i32),
            dma((6,)), dma((3,)),
            dma((PARTS, NB)), dma((PARTS, NB)),
            dma((2 * N_OFF,)), dma((2 * N_OFF,)),
            dma((PARTS, 2 * N_OFF)), dma((PARTS, 2 * N_OFF)),
            dma((PARTS, NB)), dma((PARTS, NB)),
        ],
        compiler_params=pltpu.CompilerParams(
            collective_id=0, has_side_effects=True, vmem_limit_bytes=40 << 20
        ),
    )(
        live_tiles,
        *(
            pltpu.with_memory_space_constraint(operand, pltpu.HBM)
            for operand in (
                features, weight, tiles,
                tile_source.reshape(1, TILES), tile_target.reshape(1, TILES), wanted.reshape(1, SLABS),
            )
        ),
    )


def solution(mesh):
    placed = (
        P(("row", "rep"), None),
        P(),
        P("row", "rep", None, None, None),
        P("row", "rep", None),
        P("row", "rep", None),
        P("row", "rep"),
        P("row", "rep", None, None),
    )
    return jax.shard_map(
        local, mesh=mesh, in_specs=placed, out_specs=P(("row", "rep"), None), check_vma=False
    )
```
